32 devices in a mesh: dp: 4 (over y, x), seq: 8 (over z, core).
Axes of the slice: x: 2, y: 2, z: 4, core: 2. Of those that a mesh axis runs over, the one named last changes fastest.
Arguments:
- hidden_in: bfloat16 [8, 1024, 768], P('dp', 'seq'), may hold values from -6 to 6
- lengths: int32 [8], P('dp'), may hold values from 1 to 1024, as said below
- w_attn_in: bfloat16 [2, 768, 2304], P(None, ('dp', 'seq')), may hold values from -0.21875 to 0.21875
- w_attn_out: bfloat16 [2, 768, 768], P(None, ('dp', 'seq')), may hold values from -0.875 to 0.875
- w_up: bfloat16 [2, 768, 3072], P(None, ('dp', 'seq')), may hold values from -0.21875 to 0.21875
- w_down: bfloat16 [2, 3072, 768], P(None, ('dp', 'seq')), may hold values from -0.109375 to 0.109375
- gains: bfloat16 [2, 2, 768], P(None, None, ('dp', 'seq')), may hold values from 0.25 to 1.75
- biases: bfloat16 [2, 6, 768], P(None, None, ('dp', 'seq')), may hold values from -3 to 3
- bias_hidden: bfloat16 [2, 3072], P(None, ('dp', 'seq')), may hold values from -3 to 3
- grad_out: bfloat16 [8, 1024, 768], P('dp', 'seq'), may hold values from -6 to 6
Outputs:
- hidden_out: bfloat16 [8, 1024, 768], P('dp', 'seq')
- grad_in: bfloat16 [8, 1024, 768], P('dp', 'seq')
- grad_attn_in: float32 [2, 768, 2304], P(None, ('dp', 'seq'))
- grad_attn_out: float32 [2, 768, 768], P(None, ('dp', 'seq'))
- grad_up: float32 [2, 768, 3072], P(None, ('dp', 'seq'))
- grad_down: float32 [2, 3072, 768], P(None, ('dp', 'seq'))
- grad_gains: float32 [2, 2, 768], P(None, None, ('dp', 'seq'))
- grad_biases: float32 [2, 6, 768], P(None, None, ('dp', 'seq'))
- grad_bias_hidden: float32 [2, 3072], P(None, ('dp', 'seq'))
The draws below stay inside these ranges and needn't reach their ends.
Inputs may be any that keep to these rules, and one draw needn't show every extreme that they name: `lengths`: in each group of 2 consecutive slots (one index of dp) one sequence has exactly 1024 tokens.
All inputs are finite; a program needn't handle non-finite values.
Results may differ from the reference program's by a relative error of at most 0.03.
Values may be sent and summed in bfloat16 or wider, within the bound.
A program may use at most 256 MiB of HBM per device.

```python
import math
import jax
import jax.numpy as jnp
from jax import lax

D = 768
FF = 3072
HEADS = 12
HEAD_DIM = 64
LAYERS = 2
SEQS = 2
SLOT = 1024
BATCH = 8


def draw_lengths(key, part):
    key = jax.random.fold_in(key, 11)
    groups = BATCH // SEQS
    cap_key, length_key, pick_key = jax.random.split(key, 3)
    caps = jax.random.randint(cap_key, (groups, 1), SLOT // 2, SLOT + 1)
    drawn = jax.random.randint(length_key, (groups, SEQS), jnp.maximum(caps // 2, 1), caps + 1)
    pick = jax.random.randint(pick_key, (groups, 1), 0, SEQS)
    full = jnp.arange(SEQS)[None, :] == pick
    return jnp.where(full, SLOT, drawn).reshape(BATCH).astype(jnp.int32)


def shard_levels(stream_key, dims, shards, low, largest):
    factor_of = 1.0
    for axis_at, blocks in shards:
        heights = jax.random.uniform(jax.random.fold_in(jax.random.fold_in(stream_key, 6), axis_at), (blocks,), jnp.float32, low / len(shards), largest / len(shards))
        factor_of = factor_of * jnp.repeat(jnp.exp(heights), dims[axis_at] // blocks).reshape((-1,) + (1,) * (len(dims) - 1 - axis_at))
    return factor_of


def bell_draw(key, shape, scale, bound, shards=(), kind=jnp.bfloat16):
    factor_of = shard_levels(key, shape, shards, -0.22, 0.18) if shards else 1.0
    values = jax.random.normal(key, shape, jnp.float32) * scale * factor_of
    return jnp.minimum(jnp.maximum(values, -bound), bound).astype(kind)


def setup_inputs(seed: int = 0) -> dict:
    seeds = jax.random.split(jax.random.key(seed), 11)
    hidden_in = bell_draw(seeds[0], (BATCH, SLOT, D), 1.0, 6.0, ((0, 4), (1, 8)))
    lengths = draw_lengths(jax.random.fold_in(seeds[10], 71), 0)
    w_attn_in = bell_draw(seeds[2], (LAYERS, D, 3 * D), D ** -0.5, 0.21875, ((1, 32),))
    w_attn_out = bell_draw(seeds[3], (LAYERS, D, D), (D // 16) ** -0.5, 0.875, ((1, 32),))
    w_up = bell_draw(seeds[4], (LAYERS, D, FF), D ** -0.5, 0.21875, ((1, 32),))
    w_down = bell_draw(seeds[5], (LAYERS, FF, D), FF ** -0.5, 0.109375, ((1, 32),))
    gains = jnp.clip(1.0 + 0.15 * jax.random.normal(seeds[6], (LAYERS, 2, D), jnp.float32), 0.25, 1.75).astype(jnp.bfloat16)
    biases = bell_draw(seeds[7], (LAYERS, 6, D), 0.5, 3.0, ((2, 32),))
    bias_hidden = bell_draw(seeds[8], (LAYERS, FF), 0.5, 3.0, ((1, 32),))
    grad_out = bell_draw(seeds[9], (BATCH, SLOT, D), 1.0, 6.0, ((0, 4), (1, 8)))
    return dict(hidden_in=hidden_in, lengths=lengths, w_attn_in=w_attn_in, w_attn_out=w_attn_out, w_up=w_up, w_down=w_down, gains=gains, biases=biases, bias_hidden=bias_hidden, grad_out=grad_out)


@jax.custom_vjp
def low(v):
    return lax.optimization_barrier(v.astype(jnp.bfloat16)).astype(jnp.float32)

@jax.custom_vjp
def low_back(v):
    return v

def low_keep(v):
    return (low(v), None)

def low_pass(kept, grad):
    return (grad,)

def back_keep(v):
    return (v, None)

def back_low(kept, grad):
    return (low(grad),)
low.defvjp(low_keep, low_pass)
low_back.defvjp(back_keep, back_low)
EPSILON = 1e-12
MASKED = -1000000000.0

def layer_norm(summed, gain, shift):
    center = lax.optimization_barrier(jnp.mean(summed, axis=-1, keepdims=True))
    offset = summed - center
    spread = lax.optimization_barrier(jnp.mean(offset * offset, axis=-1, keepdims=True))
    return offset * lax.rsqrt(spread + EPSILON) * gain + shift

def matmul(left, weight):
    return jnp.einsum('sqd,de->sqe', left, weight, precision=lax.Precision.HIGHEST)

def attention(query, key, value, lengths_now):
    group, span = (query.shape[0], query.shape[1])
    scale = 1.0 / math.sqrt(HEAD_DIM)
    width = math.gcd(span, 512)
    live = jnp.arange(span, dtype=jnp.int32)[None, :] < lengths_now[:, None]

    def one_block(rows):
        scores = jnp.einsum('gqhe,gkhe->ghqk', rows, key, precision=lax.Precision.HIGHEST) * scale
        scores = low_back(jnp.where(live[:, None, None, :], scores, MASKED))
        peak = lax.optimization_barrier(jnp.max(scores, axis=-1, keepdims=True))
        expo = jnp.exp(scores - peak)
        probs = low(expo / lax.optimization_barrier(jnp.sum(expo, axis=-1, keepdims=True)))
        return jnp.einsum('ghqk,gkhe->gqhe', probs, value, precision=lax.Precision.HIGHEST)
    blocks = query.reshape(group, span // width, width, HEADS, HEAD_DIM).transpose(1, 0, 2, 3, 4)
    mixed = lax.map(jax.checkpoint(one_block), blocks)
    return mixed.transpose(1, 0, 2, 3, 4).reshape(group, span, HEADS * HEAD_DIM)

def layer(state, weights, lengths_now):
    w_in, w_out, w_hid, w_back, gain, bias, bias_h = weights
    projected = matmul(low(state), w_in)
    query = low_back(low(projected[..., :D] + bias[0]))
    key = low_back(low(projected[..., D:2 * D]))
    value = low_back(low(projected[..., 2 * D:] + bias[1]))
    shape = (state.shape[0], state.shape[1], HEADS, HEAD_DIM)
    mixed = attention(query.reshape(shape), key.reshape(shape), value.reshape(shape), lengths_now)
    mixed = low_back(low(mixed))
    normed = layer_norm(state + low_back(matmul(mixed, w_out)) + bias[2], gain[0], bias[4])
    hidden = low_back(matmul(low(normed), w_hid) + bias_h)
    activated = low(jax.nn.gelu(hidden, approximate=False))
    return layer_norm(normed + low_back(matmul(activated, w_back)) + bias[3], gain[1], bias[5])

def forward(state, params, lengths_now):
    for index in range(LAYERS):
        state = layer(state, tuple((param[index] for param in params)), lengths_now)
    return state

def reference(hidden_in, lengths, w_attn_in, w_attn_out, w_up, w_down, gains, biases, bias_hidden, grad_out):
    params = tuple((param.astype(jnp.float32) for param in (w_attn_in, w_attn_out, w_up, w_down, gains, biases, bias_hidden)))
    group = math.gcd(BATCH, max(1, 4096 // SLOT))
    count = BATCH // group
    live = (jnp.arange(SLOT, dtype=jnp.int32)[None, :] < lengths[:, None]).astype(jnp.float32)
    inputs = hidden_in.astype(jnp.float32).reshape(count, group, SLOT, D)
    cotangent = (grad_out.astype(jnp.float32) * live[:, :, None]).reshape(count, group, SLOT, D)
    grouped = lengths.reshape(count, group)

    def step(totals, items):
        state, upstream, lengths_now = items
        result, pull = jax.vjp(lambda start, weights: forward(start, weights, lengths_now), state, params)
        grad_input, grad_params = pull(upstream)
        totals = jax.tree.map(jnp.add, totals, grad_params)
        return (totals, (result.astype(jnp.bfloat16), grad_input.astype(jnp.bfloat16)))
    zeros = jax.tree.map(jnp.zeros_like, params)
    totals, (results, grads) = lax.scan(step, zeros, (inputs, cotangent, grouped))
    return (results.reshape(BATCH, SLOT, D), grads.reshape(BATCH, SLOT, D), totals[0], totals[1], totals[2], totals[3], totals[4], totals[5], totals[6])
```

```python
import math

import jax
import jax.numpy as jnp
from jax import lax
from jax.sharding import PartitionSpec as P

D = 768
HEADS = 12
HEAD_DIM = 64
LAYERS = 2


EPSILON = 1e-12
MASKED = -1000000000.0


def layer_norm(summed, gain, shift):
    center = jnp.mean(summed, axis=-1, keepdims=True)
    offset = summed - center
    spread = jnp.mean(offset * offset, axis=-1, keepdims=True)
    return offset * lax.rsqrt(spread + EPSILON) * gain + shift


def norm_back(summed, gain, shift, upstream):
    _, pull = jax.vjp(layer_norm, summed, gain, shift)
    return pull(upstream)


def gelu_back(hidden, upstream):
    _, pull = jax.vjp(lambda inner: jax.nn.gelu(inner, approximate=False), hidden)
    return pull(upstream)[0]


ORDERS = {
    "in": (("seq", 1), ("dp", 2), ("dp", 1), ("seq", 2), ("seq", 4)),
    "out": (("seq", 1), ("dp", 1), ("dp", 2), ("seq", 2), ("seq", 4)),
    "up": (("seq", 1), ("dp", 1), ("seq", 2), ("dp", 2), ("seq", 4)),
    "down": (("seq", 1), ("dp", 2), ("seq", 2), ("dp", 1), ("seq", 4)),
}


def stages_of(name):
    dp, seq = lax.axis_size("dp"), lax.axis_size("seq")
    places = []
    for axis, size in (("dp", dp), ("seq", seq)):
        bit = size // 2
        while bit:
            places.append((axis, bit))
            bit //= 2
    order = [stage for stage in ORDERS[name] if stage in places]
    order += [stage for stage in places if stage not in order]
    return places, order


def swap(array, axis, bit):
    size = lax.axis_size(axis)
    return lax.ppermute(array, axis, [(i, i ^ bit) for i in range(size)])


def gather_rows(array, name):
    places, order = stages_of(name)
    held = []
    rows, columns = array.shape
    for axis, bit in reversed(order):
        at = places.index((axis, bit))
        before = 2 ** sum(places.index(other) < at for other in held)
        view = array.reshape(before, -1, columns)
        other = swap(view, axis, bit)
        high = (lax.axis_index(axis) & bit) != 0
        array = jnp.stack(
            [jnp.where(high, other, view), jnp.where(high, view, other)], axis=1
        ).reshape(-1, columns)
        held.append((axis, bit))
    return array


def scatter_rows(array, name, kind=jnp.bfloat16):
    places, order = stages_of(name)
    left = list(places)
    columns = array.shape[-1]
    array = array.astype(kind)
    for axis, bit in order:
        at = left.index((axis, bit))
        view = array.reshape(2**at, 2, -1, columns)
        high = ((lax.axis_index(axis) & bit) != 0).astype(jnp.int32)
        mine = lax.dynamic_index_in_dim(view, high, 1, keepdims=False)
        theirs = lax.dynamic_index_in_dim(view, 1 - high, 1, keepdims=False)
        total = mine.astype(jnp.float32) + swap(theirs, axis, bit).astype(jnp.float32)
        left.remove((axis, bit))
        array = total.astype(kind) if left else total
    return array.reshape(-1, columns)


def pairs_per_device(seqs):
    return -(-seqs * HEADS // lax.axis_size("seq"))


def to_pairs(array):
    seqs, block, width = array.shape
    parts = width // D
    size, per = lax.axis_size("seq"), pairs_per_device(seqs)
    turned = array.transpose(0, 2, 1).reshape(seqs, parts, HEADS, HEAD_DIM, block)
    turned = turned.transpose(0, 2, 1, 3, 4).reshape(seqs * HEADS, parts * HEAD_DIM, block)
    turned = jnp.pad(turned, ((0, size * per - seqs * HEADS), (0, 0), (0, 0)))
    moved = lax.all_to_all(
        turned.reshape(size, per, parts * HEAD_DIM, block), "seq", 0, 0, tiled=False
    )
    return moved.transpose(1, 2, 0, 3).reshape(per, parts, HEAD_DIM, size * block)


def to_rows(array, seqs):
    per, parts, _, span = array.shape
    size = lax.axis_size("seq")
    block = span // size
    turned = array.reshape(per, parts * HEAD_DIM, size, block).transpose(2, 0, 1, 3)
    moved = lax.all_to_all(turned, "seq", 0, 0, tiled=False)
    moved = moved.reshape(size * per, parts, HEAD_DIM, block)[: seqs * HEADS]
    moved = moved.reshape(seqs, HEADS, parts, HEAD_DIM, block).transpose(0, 4, 2, 1, 3)
    return moved.reshape(seqs, block, parts * D)


def scores_for(query, key, live_keys):
    raw = jnp.einsum("pfq,pfk->pqk", query, key, preferred_element_type=jnp.float32)
    return jnp.where(live_keys[:, None, :], raw * (1.0 / math.sqrt(HEAD_DIM)), MASKED)


def attend(query, key, value, live_keys):
    scores = scores_for(query, key, live_keys)
    peak = jnp.max(scores, axis=-1)
    log_total = peak + jnp.log(jnp.sum(jnp.exp(scores - peak[..., None]), axis=-1))
    probs = jnp.exp(scores - log_total[..., None]).astype(jnp.bfloat16)
    mixed = jnp.einsum("pqk,pfk->pfq", probs, value, preferred_element_type=jnp.float32)
    return (log_total, mixed)


def attend_back(query, key, value, live_keys, log_total, mixed_full, mixed_grad):
    scale = 1.0 / math.sqrt(HEAD_DIM)
    delta = jnp.sum(mixed_grad.astype(jnp.float32) * mixed_full, axis=1)
    probs = jnp.exp(scores_for(query, key, live_keys) - log_total[..., None])
    grad_probs = jnp.einsum("pfq,pfk->pqk", mixed_grad, value, preferred_element_type=jnp.float32)
    grad_scores = (probs * (grad_probs - delta[..., None])).astype(jnp.bfloat16)
    probs = probs.astype(jnp.bfloat16)
    query_grad = (
        jnp.einsum("pqk,pfk->pfq", grad_scores, key, preferred_element_type=jnp.float32) * scale
    )
    key_grad = (
        jnp.einsum("pqk,pfq->pfk", grad_scores, query, preferred_element_type=jnp.float32) * scale
    )
    value_grad = jnp.einsum("pqk,pfq->pfk", probs, mixed_grad, preferred_element_type=jnp.float32)
    return jnp.stack([query_grad, key_grad, value_grad], axis=1).astype(jnp.bfloat16)


def forward_layer(state, weights, live_keys):
    w_in, w_out, w_hid, w_back, gain, bias, bias_h = weights
    gain = gain.astype(jnp.float32)
    bias = bias.astype(jnp.float32)
    bias_h = bias_h.astype(jnp.float32)
    lowered = state.astype(jnp.bfloat16)
    projected = jnp.dot(lowered, w_in, preferred_element_type=jnp.float32)
    query = (projected[..., :D] + bias[0]).astype(jnp.bfloat16)
    key = projected[..., D : 2 * D].astype(jnp.bfloat16)
    value = (projected[..., 2 * D :] + bias[1]).astype(jnp.bfloat16)
    pairs = to_pairs(jnp.concatenate((query, key, value), axis=-1))
    log_total, mixed_full = attend(pairs[:, 0], pairs[:, 1], pairs[:, 2], live_keys)
    mixed = to_rows(mixed_full.astype(jnp.bfloat16)[:, None], state.shape[0])
    first_sum = state + (jnp.dot(mixed, w_out, preferred_element_type=jnp.float32) + bias[2])
    normed = layer_norm(first_sum, gain[0], bias[4])
    normed_low = normed.astype(jnp.bfloat16)
    hidden = jnp.dot(normed_low, w_hid, preferred_element_type=jnp.float32) + bias_h
    activated = jax.nn.gelu(hidden, approximate=False).astype(jnp.bfloat16)
    second_sum = normed + (jnp.dot(activated, w_back, preferred_element_type=jnp.float32) + bias[3])
    result = layer_norm(second_sum, gain[1], bias[5])
    saved = (
        lowered,
        pairs,
        log_total,
        mixed_full,
        mixed,
        first_sum,
        normed_low,
        hidden,
        activated,
        second_sum,
    )
    return (result, saved)


def backward_layer(upstream, weights, saved, live_keys):
    w_in, w_out, w_hid, w_back, gain, bias, bias_h = weights
    gain = gain.astype(jnp.float32)
    bias = bias.astype(jnp.float32)
    (
        lowered,
        pairs,
        log_total,
        mixed_full,
        mixed,
        first_sum,
        normed_low,
        hidden,
        activated,
        second_sum,
    ) = saved
    grad_second, grad_gain_two, grad_shift_two = norm_back(second_sum, gain[1], bias[5], upstream)
    down_grad = grad_second.astype(jnp.bfloat16)
    grad_bias_down = jnp.sum(grad_second, axis=(0, 1))
    grad_down_w = jnp.einsum(
        "sqf,sqd->fd", activated, down_grad, preferred_element_type=jnp.float32
    )
    grad_activated = jnp.einsum(
        "sqd,fd->sqf", down_grad, w_back, preferred_element_type=jnp.float32
    )
    hidden_grad = gelu_back(hidden, grad_activated).astype(jnp.bfloat16)
    grad_bias_h = jnp.sum(hidden_grad.astype(jnp.float32), axis=(0, 1))
    grad_up_w = jnp.einsum(
        "sqd,sqf->df", normed_low, hidden_grad, preferred_element_type=jnp.float32
    )
    grad_normed = grad_second + jnp.einsum(
        "sqf,df->sqd", hidden_grad, w_hid, preferred_element_type=jnp.float32
    )
    grad_first, grad_gain_one, grad_shift_one = norm_back(first_sum, gain[0], bias[4], grad_normed)
    out_grad = grad_first.astype(jnp.bfloat16)
    grad_bias_out = jnp.sum(grad_first, axis=(0, 1))
    grad_out_w = jnp.einsum("sqd,sqe->de", mixed, out_grad, preferred_element_type=jnp.float32)
    mixed_grad = jnp.einsum(
        "sqe,de->sqd", out_grad, w_out, preferred_element_type=jnp.float32
    ).astype(jnp.bfloat16)
    pairs_grad = attend_back(
        pairs[:, 0],
        pairs[:, 1],
        pairs[:, 2],
        live_keys,
        log_total,
        mixed_full,
        to_pairs(mixed_grad)[:, 0],
    )
    projected_grad = to_rows(pairs_grad, mixed_grad.shape[0])
    grad_bias_query = jnp.sum(projected_grad[..., :D].astype(jnp.float32), axis=(0, 1))
    grad_bias_value = jnp.sum(projected_grad[..., 2 * D :].astype(jnp.float32), axis=(0, 1))
    grad_in_w = jnp.einsum(
        "sqd,sqe->de", lowered, projected_grad, preferred_element_type=jnp.float32
    )
    grad_state = grad_first + jnp.einsum(
        "sqe,de->sqd", projected_grad, w_in, preferred_element_type=jnp.float32
    )
    grad_gains_now = jnp.stack([grad_gain_one, grad_gain_two])
    grad_biases_now = jnp.stack(
        [
            grad_bias_query,
            grad_bias_value,
            grad_bias_out,
            grad_bias_down,
            grad_shift_one,
            grad_shift_two,
        ]
    )
    terms = (
        grad_in_w,
        grad_out_w,
        grad_up_w,
        grad_down_w,
        grad_gains_now,
        grad_biases_now,
        grad_bias_h,
    )
    return (grad_state, terms)


def per_device(
    hidden_in, lengths, w_attn_in, w_attn_out, w_up, w_down, gains, biases, bias_hidden, grad_out
):
    seqs, block, width = hidden_in.shape
    span = block * lax.axis_size("seq")
    first_row = lax.axis_index("seq") * block
    per = pairs_per_device(seqs)
    first_pair = lax.axis_index("seq") * per
    sequence_of = jnp.minimum((first_pair + jnp.arange(per, dtype=jnp.int32)) // HEADS, seqs - 1)
    pair_lengths = jnp.take(lengths, sequence_of)
    live_keys = jnp.arange(span, dtype=jnp.int32)[None, :] < pair_lengths[:, None]
    live_rows = (
        (first_row + jnp.arange(block, dtype=jnp.int32))[None, :] < lengths[:, None]
    ).astype(jnp.float32)
    state = hidden_in.astype(jnp.float32)
    devices = lax.axis_size("dp") * lax.axis_size("seq")
    thin = gains.shape[2]
    small = jnp.concatenate(
        [gains.reshape(LAYERS, -1), biases.reshape(LAYERS, -1), bias_hidden], axis=1
    ).reshape(1, -1)
    small = gather_rows(small, "in").reshape(devices, LAYERS, -1)
    split = 2 * thin
    stored = []
    for layer in range(LAYERS):
        weights = (
            gather_rows(w_attn_in[layer], "in"),
            gather_rows(w_attn_out[layer], "out"),
            gather_rows(w_up[layer], "up"),
            gather_rows(w_down[layer], "down"),
            small[:, layer, :split].reshape(devices, 2, thin).transpose(1, 0, 2).reshape(2, D),
            small[:, layer, split : 4 * split]
            .reshape(devices, 6, thin)
            .transpose(1, 0, 2)
            .reshape(6, D),
            small[:, layer, 4 * split :].reshape(-1),
        )
        state, saved = forward_layer(state, weights, live_keys)
        stored.append((weights, saved))
    upstream = grad_out.astype(jnp.float32) * live_rows[..., None]
    collected = []
    for layer in reversed(range(LAYERS)):
        weights, saved = stored[layer]
        upstream, terms = backward_layer(upstream, weights, saved, live_keys)
        thin_terms = jnp.concatenate(
            [
                terms[4].reshape(2, devices, thin).transpose(1, 0, 2).reshape(devices, -1),
                terms[5].reshape(6, devices, thin).transpose(1, 0, 2).reshape(devices, -1),
                terms[6].reshape(devices, -1),
            ],
            axis=1,
        )
        summed = scatter_rows(thin_terms, "out", jnp.float32)[0]
        collected.insert(
            0,
            (
                scatter_rows(terms[0], "in"),
                scatter_rows(terms[1], "out"),
                scatter_rows(terms[2], "up"),
                scatter_rows(terms[3], "down"),
                summed[:split].reshape(2, thin),
                summed[split : 4 * split].reshape(6, thin),
                summed[4 * split :],
            ),
        )
    stacked = tuple((jnp.stack([shares[member] for shares in collected]) for member in range(7)))
    return (state.astype(jnp.bfloat16), upstream.astype(jnp.bfloat16)) + stacked


def solution(mesh):
    placed = (
        P("dp", "seq", None),
        P("dp"),
        P(None, ("dp", "seq"), None),
        P(None, ("dp", "seq"), None),
        P(None, ("dp", "seq"), None),
        P(None, ("dp", "seq"), None),
        P(None, None, ("dp", "seq")),
        P(None, None, ("dp", "seq")),
        P(None, ("dp", "seq")),
        P("dp", "seq", None),
    )
    return jax.shard_map(
        per_device,
        mesh=mesh,
        in_specs=placed,
        out_specs=(
            P("dp", "seq", None),
            P("dp", "seq", None),
            P(None, ("dp", "seq"), None),
            P(None, ("dp", "seq"), None),
            P(None, ("dp", "seq"), None),
            P(None, ("dp", "seq"), None),
            P(None, None, ("dp", "seq")),
            P(None, None, ("dp", "seq")),
            P(None, ("dp", "seq")),
        ),
        check_vma=False,
    )
```

```python
import math

import jax
import jax.numpy as jnp
from jax import lax
from jax.sharding import PartitionSpec as P

D = 768
HEADS = 12
HEAD_DIM = 64
LAYERS = 2


EPSILON = 1e-12
MASKED = -1000000000.0


def layer_norm(summed, gain, shift):
    center = jnp.mean(summed, axis=-1, keepdims=True)
    offset = summed - center
    spread = jnp.mean(offset * offset, axis=-1, keepdims=True)
    return offset * lax.rsqrt(spread + EPSILON) * gain + shift


def norm_back(summed, gain, shift, upstream):
    _, pull = jax.vjp(layer_norm, summed, gain, shift)
    return pull(upstream)


def gelu_back(hidden, upstream):
    _, pull = jax.vjp(lambda inner: jax.nn.gelu(inner, approximate=False), hidden)
    return pull(upstream)[0]


ORDERS = {
    "in": (("seq", 1), ("dp", 2), ("dp", 1), ("seq", 2), ("seq", 4)),
    "out": (("seq", 1), ("dp", 1), ("dp", 2), ("seq", 2), ("seq", 4)),
    "up": (("seq", 1), ("dp", 1), ("seq", 2), ("dp", 2), ("seq", 4)),
    "down": (("seq", 1), ("dp", 2), ("seq", 2), ("dp", 1), ("seq", 4)),
}


def stages_of(name):
    dp, seq = lax.axis_size("dp"), lax.axis_size("seq")
    places = []
    for axis, size in (("dp", dp), ("seq", seq)):
        bit = size // 2
        while bit:
            places.append((axis, bit))
            bit //= 2
    order = [stage for stage in ORDERS[name] if stage in places]
    order += [stage for stage in places if stage not in order]
    return places, order


def swap(array, axis, bit):
    size = lax.axis_size(axis)
    return lax.ppermute(array, axis, [(i, i ^ bit) for i in range(size)])


def gather_rows(array, name):
    places, order = stages_of(name)
    held = []
    rows, columns = array.shape
    for axis, bit in reversed(order):
        at = places.index((axis, bit))
        before = 2 ** sum(places.index(other) < at for other in held)
        view = array.reshape(before, -1, columns)
        other = swap(view, axis, bit)
        high = (lax.axis_index(axis) & bit) != 0
        array = jnp.stack(
            [jnp.where(high, other, view), jnp.where(high, view, other)], axis=1
        ).reshape(-1, columns)
        held.append((axis, bit))
    return array


def scatter_rows(array, name, kind=jnp.bfloat16):
    places, order = stages_of(name)
    left = list(places)
    columns = array.shape[-1]
    array = array.astype(kind)
    for axis, bit in order:
        at = left.index((axis, bit))
        view = array.reshape(2**at, 2, -1, columns)
        high = ((lax.axis_index(axis) & bit) != 0).astype(jnp.int32)
        mine = lax.dynamic_index_in_dim(view, high, 1, keepdims=False)
        theirs = lax.dynamic_index_in_dim(view, 1 - high, 1, keepdims=False)
        total = mine.astype(jnp.float32) + swap(theirs, axis, bit).astype(jnp.float32)
        left.remove((axis, bit))
        array = total.astype(kind) if left else total
    return array.reshape(-1, columns)


def after(array, done):
    return lax.optimization_barrier((array, done))


def pairs_per_device(seqs):
    return -(-seqs * HEADS // lax.axis_size("seq"))


def to_pairs(array):
    seqs, block, width = array.shape
    parts = width // D
    size, per = lax.axis_size("seq"), pairs_per_device(seqs)
    turned = array.transpose(0, 2, 1).reshape(seqs, parts, HEADS, HEAD_DIM, block)
    turned = turned.transpose(0, 2, 1, 3, 4).reshape(seqs * HEADS, parts * HEAD_DIM, block)
    turned = jnp.pad(turned, ((0, size * per - seqs * HEADS), (0, 0), (0, 0)))
    moved = lax.all_to_all(
        turned.reshape(size, per, parts * HEAD_DIM, block), "seq", 0, 0, tiled=False
    )
    return moved.transpose(1, 2, 0, 3).reshape(per, parts, HEAD_DIM, size * block)


def to_rows(array, seqs):
    per, parts, _, span = array.shape
    size = lax.axis_size("seq")
    block = span // size
    turned = array.reshape(per, parts * HEAD_DIM, size, block).transpose(2, 0, 1, 3)
    moved = lax.all_to_all(turned, "seq", 0, 0, tiled=False)
    moved = moved.reshape(size * per, parts, HEAD_DIM, block)[: seqs * HEADS]
    moved = moved.reshape(seqs, HEADS, parts, HEAD_DIM, block).transpose(0, 4, 2, 1, 3)
    return moved.reshape(seqs, block, parts * D)


def scores_for(query, key, live_keys):
    raw = jnp.einsum("pfq,pfk->pqk", query, key, preferred_element_type=jnp.float32)
    return jnp.where(live_keys[:, None, :], raw * (1.0 / math.sqrt(HEAD_DIM)), MASKED)


def attend(query, key, value, live_keys):
    scores = scores_for(query, key, live_keys)
    peak = jnp.max(scores, axis=-1)
    log_total = peak + jnp.log(jnp.sum(jnp.exp(scores - peak[..., None]), axis=-1))
    probs = jnp.exp(scores - log_total[..., None]).astype(jnp.bfloat16)
    mixed = jnp.einsum("pqk,pfk->pfq", probs, value, preferred_element_type=jnp.float32)
    return (log_total, mixed)


def attend_back(query, key, value, live_keys, log_total, mixed_full, mixed_grad):
    scale = 1.0 / math.sqrt(HEAD_DIM)
    delta = jnp.sum(mixed_grad.astype(jnp.float32) * mixed_full, axis=1)
    probs = jnp.exp(scores_for(query, key, live_keys) - log_total[..., None])
    grad_probs = jnp.einsum("pfq,pfk->pqk", mixed_grad, value, preferred_element_type=jnp.float32)
    grad_scores = (probs * (grad_probs - delta[..., None])).astype(jnp.bfloat16)
    probs = probs.astype(jnp.bfloat16)
    query_grad = (
        jnp.einsum("pqk,pfk->pfq", grad_scores, key, preferred_element_type=jnp.float32) * scale
    )
    key_grad = (
        jnp.einsum("pqk,pfq->pfk", grad_scores, query, preferred_element_type=jnp.float32) * scale
    )
    value_grad = jnp.einsum("pqk,pfq->pfk", probs, mixed_grad, preferred_element_type=jnp.float32)
    return jnp.stack([query_grad, key_grad, value_grad], axis=1).astype(jnp.bfloat16)


def forward_layer(state, weights, live_keys):
    w_in, w_out, w_hid, w_back, gain, bias, bias_h = weights
    gain = gain.astype(jnp.float32)
    bias = bias.astype(jnp.float32)
    bias_h = bias_h.astype(jnp.float32)
    lowered = state.astype(jnp.bfloat16)
    projected = jnp.dot(lowered, w_in, preferred_element_type=jnp.float32)
    query = (projected[..., :D] + bias[0]).astype(jnp.bfloat16)
    key = projected[..., D : 2 * D].astype(jnp.bfloat16)
    value = (projected[..., 2 * D :] + bias[1]).astype(jnp.bfloat16)
    pairs = to_pairs(jnp.concatenate((query, key, value), axis=-1))
    log_total, mixed_full = attend(pairs[:, 0], pairs[:, 1], pairs[:, 2], live_keys)
    mixed = to_rows(mixed_full.astype(jnp.bfloat16)[:, None], state.shape[0])
    first_sum = state + (jnp.dot(mixed, w_out, preferred_element_type=jnp.float32) + bias[2])
    normed = layer_norm(first_sum, gain[0], bias[4])
    normed_low = normed.astype(jnp.bfloat16)
    hidden = jnp.dot(normed_low, w_hid, preferred_element_type=jnp.float32) + bias_h
    activated = jax.nn.gelu(hidden, approximate=False).astype(jnp.bfloat16)
    second_sum = normed + (jnp.dot(activated, w_back, preferred_element_type=jnp.float32) + bias[3])
    result = layer_norm(second_sum, gain[1], bias[5])
    saved = (
        lowered,
        pairs,
        log_total,
        mixed_full,
        mixed,
        first_sum,
        normed_low,
        hidden,
        activated,
        second_sum,
    )
    return (result, saved)


def backward_layer(upstream, weights, saved, live_keys, finished):
    w_in, w_out, w_hid, w_back, gain, bias, bias_h = weights
    gain = gain.astype(jnp.float32)
    bias = bias.astype(jnp.float32)
    (
        lowered,
        pairs,
        log_total,
        mixed_full,
        mixed,
        first_sum,
        normed_low,
        hidden,
        activated,
        second_sum,
    ) = saved
    grad_second, grad_gain_two, grad_shift_two = norm_back(second_sum, gain[1], bias[5], upstream)
    down_grad = grad_second.astype(jnp.bfloat16)
    grad_bias_down = jnp.sum(grad_second, axis=(0, 1))
    grad_down_w = jnp.einsum(
        "sqf,sqd->fd", activated, down_grad, preferred_element_type=jnp.float32
    )
    grad_activated = jnp.einsum(
        "sqd,fd->sqf", down_grad, w_back, preferred_element_type=jnp.float32
    )
    hidden_grad = gelu_back(hidden, grad_activated).astype(jnp.bfloat16)
    grad_bias_h = jnp.sum(hidden_grad.astype(jnp.float32), axis=(0, 1))
    grad_up_w = jnp.einsum(
        "sqd,sqf->df", normed_low, hidden_grad, preferred_element_type=jnp.float32
    )
    grad_normed = grad_second + jnp.einsum(
        "sqf,df->sqd", hidden_grad, w_hid, preferred_element_type=jnp.float32
    )
    grad_first, grad_gain_one, grad_shift_one = norm_back(first_sum, gain[0], bias[4], grad_normed)
    out_grad = grad_first.astype(jnp.bfloat16)
    grad_bias_out = jnp.sum(grad_first, axis=(0, 1))
    grad_out_w = jnp.einsum("sqd,sqe->de", mixed, out_grad, preferred_element_type=jnp.float32)
    mixed_grad = jnp.einsum(
        "sqe,de->sqd", out_grad, w_out, preferred_element_type=jnp.float32
    ).astype(jnp.bfloat16)
    mixed_pairs = to_pairs(mixed_grad)[:, 0]
    if finished is not None:
        mixed_pairs, finished = after(mixed_pairs, finished)
    pairs_grad = attend_back(
        pairs[:, 0],
        pairs[:, 1],
        pairs[:, 2],
        live_keys,
        log_total,
        mixed_full,
        mixed_pairs,
    )
    projected_grad = to_rows(pairs_grad, mixed_grad.shape[0])
    grad_bias_query = jnp.sum(projected_grad[..., :D].astype(jnp.float32), axis=(0, 1))
    grad_bias_value = jnp.sum(projected_grad[..., 2 * D :].astype(jnp.float32), axis=(0, 1))
    grad_in_w = jnp.einsum(
        "sqd,sqe->de", lowered, projected_grad, preferred_element_type=jnp.float32
    )
    grad_state = grad_first + jnp.einsum(
        "sqe,de->sqd", projected_grad, w_in, preferred_element_type=jnp.float32
    )
    grad_gains_now = jnp.stack([grad_gain_one, grad_gain_two])
    grad_biases_now = jnp.stack(
        [
            grad_bias_query,
            grad_bias_value,
            grad_bias_out,
            grad_bias_down,
            grad_shift_one,
            grad_shift_two,
        ]
    )
    terms = (
        grad_in_w,
        grad_out_w,
        grad_up_w,
        grad_down_w,
        grad_gains_now,
        grad_biases_now,
        grad_bias_h,
    )
    return (grad_state, terms, finished)


def per_device(
    hidden_in, lengths, w_attn_in, w_attn_out, w_up, w_down, gains, biases, bias_hidden, grad_out
):
    seqs, block, width = hidden_in.shape
    span = block * lax.axis_size("seq")
    first_row = lax.axis_index("seq") * block
    per = pairs_per_device(seqs)
    first_pair = lax.axis_index("seq") * per
    sequence_of = jnp.minimum((first_pair + jnp.arange(per, dtype=jnp.int32)) // HEADS, seqs - 1)
    pair_lengths = jnp.take(lengths, sequence_of)
    live_keys = jnp.arange(span, dtype=jnp.int32)[None, :] < pair_lengths[:, None]
    live_rows = (
        (first_row + jnp.arange(block, dtype=jnp.int32))[None, :] < lengths[:, None]
    ).astype(jnp.float32)
    state = hidden_in.astype(jnp.float32)
    devices = lax.axis_size("dp") * lax.axis_size("seq")
    thin = gains.shape[2]
    small = jnp.concatenate(
        [gains.reshape(LAYERS, -1), biases.reshape(LAYERS, -1), bias_hidden], axis=1
    ).reshape(1, -1)
    small = gather_rows(small, "in").reshape(devices, LAYERS, -1)
    split = 2 * thin
    stored = []
    ready = None
    for layer in range(LAYERS):
        shard_in = w_attn_in[layer]
        if ready is not None:
            shard_in, _ = after(shard_in, ready)
        full_in = gather_rows(shard_in, "in")
        (shard_out, shard_up, shard_down), full_in = after(
            (w_attn_out[layer], w_up[layer], w_down[layer]), full_in
        )
        weights = (
            full_in,
            gather_rows(shard_out, "out"),
            gather_rows(shard_up, "up"),
            gather_rows(shard_down, "down"),
            small[:, layer, :split].reshape(devices, 2, thin).transpose(1, 0, 2).reshape(2, D),
            small[:, layer, split : 4 * split]
            .reshape(devices, 6, thin)
            .transpose(1, 0, 2)
            .reshape(6, D),
            small[:, layer, 4 * split :].reshape(-1),
        )
        state, saved = forward_layer(state, weights, live_keys)
        ready = saved[2]
        stored.append((weights, saved))
    upstream = grad_out.astype(jnp.float32) * live_rows[..., None]
    collected = []
    for layer in reversed(range(LAYERS)):
        weights, saved = stored[layer]
        finished = collected[0] if collected else None
        upstream, terms, finished = backward_layer(upstream, weights, saved, live_keys, finished)
        if collected:
            collected[0] = finished
        thin_terms = jnp.concatenate(
            [
                terms[4].reshape(2, devices, thin).transpose(1, 0, 2).reshape(devices, -1),
                terms[5].reshape(6, devices, thin).transpose(1, 0, 2).reshape(devices, -1),
                terms[6].reshape(devices, -1),
            ],
            axis=1,
        )
        summed = scatter_rows(thin_terms, "out", jnp.float32)[0]
        collected.insert(
            0,
            (
                scatter_rows(terms[0], "in"),
                scatter_rows(terms[1], "out"),
                scatter_rows(terms[2], "up"),
                scatter_rows(terms[3], "down"),
                summed[:split].reshape(2, thin),
                summed[split : 4 * split].reshape(6, thin),
                summed[4 * split :],
            ),
        )
    stacked = tuple((jnp.stack([shares[member] for shares in collected]) for member in range(7)))
    return (state.astype(jnp.bfloat16), upstream.astype(jnp.bfloat16)) + stacked


def solution(mesh):
    placed = (
        P("dp", "seq", None),
        P("dp"),
        P(None, ("dp", "seq"), None),
        P(None, ("dp", "seq"), None),
        P(None, ("dp", "seq"), None),
        P(None, ("dp", "seq"), None),
        P(None, None, ("dp", "seq")),
        P(None, None, ("dp", "seq")),
        P(None, ("dp", "seq")),
        P("dp", "seq", None),
    )
    return jax.shard_map(
        per_device,
        mesh=mesh,
        in_specs=placed,
        out_specs=(
            P("dp", "seq", None),
            P("dp", "seq", None),
            P(None, ("dp", "seq"), None),
            P(None, ("dp", "seq"), None),
            P(None, ("dp", "seq"), None),
            P(None, ("dp", "seq"), None),
            P(None, None, ("dp", "seq")),
            P(None, None, ("dp", "seq")),
            P(None, ("dp", "seq")),
        ),
        check_vma=False,
    )
```
